1024 devices in a mesh: group: 8 (over x_lo, core), node: 16 (over x_hi, y), chip: 8 (over z).
Axes of the slice: x: 8 (x_hi: 2, x_lo: 4; x = x_hi * 4 + x_lo), y: 8, z: 8, core: 2. Of those that a mesh axis runs over, the one named last changes fastest.
Arguments:
- prompt_cache: bfloat16 [8, 16, 4, 192, 576], P('group', 'node', None, 'chip'), may hold values from -4 to 4
- prompt_lengths: int32 [8, 16, 4], replicated, may hold values from 1 to 192, 480 in all within a row
- prompt_replica: int32 [8, 16, 4], replicated, may hold values from 0 to 15, as said below
- new_queries: bfloat16 [8, 16, 16, 2, 128, 576], P('group', 'node', None, None, 'chip'), may hold values from -32 to 32
- new_rows: bfloat16 [8, 16, 16, 2, 576], P('group', 'node'), may hold values from -4 to 4
- resident_cache: bfloat16 [8, 16, 3, 1024, 576], P('group', 'node'), may hold values from -4 to 4
- resident_queries: bfloat16 [8, 16, 3, 2, 128, 576], P('group', 'node', None, None, 'chip'), may hold values from -32 to 32
- resident_rows: bfloat16 [8, 16, 3, 2, 576], P('group', 'node'), may hold values from -4 to 4
- resident_lengths: int32 [8, 16, 3], P('group', 'node'), may hold values from 1 to 1024, 1920 in all within a row
Outputs:
- new_context: bfloat16 [8, 16, 16, 2, 128, 512], P('group', 'node', None, None, 'chip')
- resident_context: bfloat16 [8, 16, 3, 2, 128, 512], P('group', 'node', None, None, 'chip')
The draws below stay inside these ranges and needn't reach their ends.
Inputs may be any that keep to these rules, and one draw needn't show every extreme that they name: `prompt_replica`: the 4 prompts of one prefill node go to different replicas; one replica may receive prompts from any number of prefill nodes.
All inputs are finite; a program needn't handle non-finite values.
Results may differ from the reference program's by a relative error of at most 0.0034.
Values may be sent and summed in bfloat16 or wider, within the bound.
No kernel may reach another device: no remote copies, remote signals or barrier semaphores. Data moves between devices by JAX's collectives and lax.ppermute only.
A program may use at most 64 MiB of HBM per device.

```python
import math
import jax
import jax.numpy as jnp
import numpy as np
from jax import lax

HEADS = 128
LATENT = 512
CW = 576
STEPS = 2
LEN = 192
PRN = 4
RES = 3
RLEN = 1024
N_GROUP = 8
N_NODE = 16


def latent_values(seed_key, array_shape):
    return jnp.clip(jax.random.normal(seed_key, array_shape, jnp.float32), -4.0, 4.0)


def first_rows(seed_key, lead_shape):
    return latent_values(jax.random.fold_in(seed_key, 1), lead_shape + (1, CW))


def cache_with_first(seed_key, lead_shape, row_count):
    first_row = first_rows(seed_key, lead_shape)
    later_rows = latent_values(jax.random.fold_in(seed_key, 2), lead_shape + (row_count - 1, CW))
    return jnp.concatenate([first_row, later_rows], axis=-2)


def replica_table(seed_key):
    jitter_key, favour_key = jax.random.split(seed_key)
    jitter = jax.random.randint(jitter_key, (N_GROUP, N_NODE, N_NODE), 0, 2 ** 20)
    favour = jax.random.randint(favour_key, (N_GROUP, 1, N_NODE), 0, 3) * 2 ** 19
    scores = (jitter + favour) * N_NODE + lax.broadcasted_iota(jnp.int32, (N_GROUP, N_NODE, N_NODE), 2)
    ranked = jnp.argsort(-scores, axis=-1)
    return ranked[..., :PRN].astype(jnp.int32)


def draw_prompt_cache(key, part):
    return cache_with_first(jax.random.fold_in(key, 11), (N_GROUP, N_NODE, PRN), LEN).astype(jnp.bfloat16)


def draw_prompt_replica(key, part):
    return replica_table(jax.random.fold_in(key, 7))


def draw_new_rows(key, part):
    return latent_values(jax.random.fold_in(key, 41), (N_GROUP, N_NODE, N_NODE, STEPS, CW)).astype(jnp.bfloat16)


def draw_new_queries(key, part):
    drawn_part = jnp.clip(jax.random.normal(jax.random.fold_in(key, 31), (N_GROUP, N_NODE, N_NODE, STEPS, HEADS, CW), jnp.float32), -4.0, 4.0)
    return drawn_part.astype(jnp.bfloat16)


def draw_resident_cache(key, part):
    return cache_with_first(jax.random.fold_in(key, 51), (N_GROUP, N_NODE, RES), RLEN).astype(jnp.bfloat16)


def draw_resident_rows(key, part):
    return latent_values(jax.random.fold_in(key, 61), (N_GROUP, N_NODE, RES, STEPS, CW)).astype(jnp.bfloat16)


def draw_resident_queries(key, part):
    drawn_part = jnp.clip(jax.random.normal(jax.random.fold_in(key, 71), (N_GROUP, N_NODE, RES, STEPS, HEADS, CW), jnp.float32), -4.0, 4.0)
    return drawn_part.astype(jnp.bfloat16)


def length_profile(amount, total, reach, skew):
    loads = [(1 << 20) // math.isqrt(rank ** skew) + 1 for rank in range(2, amount + 1)]
    surplus, holding = total - reach - (amount - 1), [1] * (amount - 1)
    while surplus > 0:
        movable = [i for i in range(amount - 1) if holding[i] < reach]
        mass, remaining = sum([loads[i] for i in movable]), surplus
        for i in movable:
            more = min(reach - holding[i], max(1, remaining * loads[i] // mass), surplus)
            holding[i] = holding[i] + more
            surplus = surplus - more
    return np.array([reach] + holding)


def uneven_parts(key, count, total, bound, slope):
    if count == 2:
        one = jax.random.randint(key, (), max(1, total - bound), min(bound, total - 1) + 1)
        return jnp.stack([one, total - one])
    sizes = jnp.asarray(length_profile(count, total, bound, slope), jnp.int32)
    twos = (count - 1) // 2
    giver, receiver = sizes[1:1 + 2 * twos:2], sizes[2:2 + 2 * twos:2]
    margin = jnp.minimum(giver - 1, bound - receiver)
    shifted = jax.random.randint(jax.random.fold_in(key, 1), (twos,), 0, 1 << 20) % (margin + 1)
    sizes = sizes.at[1:1 + 2 * twos:2].set(giver - shifted).at[2:2 + 2 * twos:2].set(receiver + shifted)
    return sizes[jax.random.permutation(jax.random.fold_in(key, 2), count)]


def setup_inputs(seed: int = 0) -> dict:
    splits = jax.random.split(jax.random.key(seed), 10)
    return {
        "prompt_cache": draw_prompt_cache(jax.random.fold_in(splits[9], 71), 0),
        "prompt_lengths": jax.vmap(lambda own: uneven_parts(own, PRN, PRN * LEN * 5 // 8, LEN, 1))(jax.random.split(splits[1], N_GROUP * N_NODE)).reshape((N_GROUP, N_NODE, PRN)).astype(jnp.int32),
        "prompt_replica": draw_prompt_replica(jax.random.fold_in(splits[9], 71), 0),
        "new_queries": draw_new_queries(jax.random.fold_in(splits[9], 71), 0),
        "new_rows": draw_new_rows(jax.random.fold_in(splits[9], 71), 0),
        "resident_cache": draw_resident_cache(jax.random.fold_in(splits[9], 71), 0),
        "resident_queries": draw_resident_queries(jax.random.fold_in(splits[9], 71), 0),
        "resident_rows": draw_resident_rows(jax.random.fold_in(splits[9], 71), 0),
        "resident_lengths": jax.vmap(lambda own: uneven_parts(own, RES, RES * RLEN * 5 // 8, RLEN, 1))(jax.random.split(splits[8], N_GROUP * N_NODE)).reshape((N_GROUP, N_NODE, RES)).astype(jnp.int32),
    }


score_scale = 1.0 / 192.0 ** 0.5


def scores_of(queries, keys_block):
    return jnp.einsum("bshc,blc->bshl", queries.astype(jnp.float32), keys_block.astype(jnp.float32), precision=lax.Precision.HIGHEST) * score_scale


def attend_all(queries, keys_cache, own_rows, lengths):
    step_count = own_rows.shape[1]
    cache_pos = lax.broadcasted_iota(jnp.int32, (1, 1, 1, keys_cache.shape[1]), 3)
    cache_ok = cache_pos < lengths.astype(jnp.int32)[:, None, None, None]
    step_here = lax.broadcasted_iota(jnp.int32, (1, step_count, 1, step_count), 1)
    own_here = lax.broadcasted_iota(jnp.int32, (1, step_count, 1, step_count), 3)
    own_ok = own_here <= step_here
    cache_scores = jnp.where(cache_ok, scores_of(queries, keys_cache), -jnp.inf)
    own_scores = jnp.where(own_ok, scores_of(queries, own_rows), -jnp.inf)
    row_top = jnp.maximum(jnp.max(cache_scores, axis=3), jnp.max(own_scores, axis=3))
    cache_exp = jnp.exp(cache_scores - row_top[..., None])
    own_exp = jnp.exp(own_scores - row_top[..., None])
    row_total = jnp.sum(cache_exp, axis=3) + jnp.sum(own_exp, axis=3)
    cache_weights = lax.optimization_barrier(cache_exp.astype(jnp.bfloat16)).astype(jnp.float32)
    own_weights = lax.optimization_barrier(own_exp.astype(jnp.bfloat16)).astype(jnp.float32)
    numerator = jnp.einsum("bshl,bld->bshd", cache_weights, keys_cache[:, :, :LATENT].astype(jnp.float32), precision=lax.Precision.HIGHEST)
    numerator = numerator + jnp.einsum("bshl,bld->bshd", own_weights, own_rows[:, :, :LATENT].astype(jnp.float32), precision=lax.Precision.HIGHEST)
    return numerator / row_total[..., None]


def reference(prompt_cache, prompt_lengths, prompt_replica, new_queries, new_rows, resident_cache, resident_queries, resident_rows, resident_lengths):
    group_count = prompt_cache.shape[0]
    node_count = prompt_cache.shape[1]

    def one_replica(replica_index):
        group_here = replica_index // node_count
        node_here = replica_index % node_count
        source_group = (group_here + group_count - group_count // 2) % group_count
        source_table = prompt_replica[source_group]
        chosen = source_table == node_here
        is_live = jnp.any(chosen, axis=1)
        picked = jnp.argmax(chosen.astype(jnp.int32), axis=1).astype(jnp.int32)
        slot_lengths = jnp.sum(jnp.where(chosen, prompt_lengths[source_group], 0), axis=1).astype(jnp.int32)
        slot_caches = prompt_cache[source_group][jnp.arange(node_count, dtype=jnp.int32), picked]
        context = attend_all(new_queries[group_here, node_here], slot_caches, new_rows[group_here, node_here], slot_lengths)
        context = context * is_live.astype(jnp.float32)[:, None, None, None]
        standing = attend_all(resident_queries[group_here, node_here], resident_cache[group_here, node_here], resident_rows[group_here, node_here], resident_lengths[group_here, node_here])
        return context.astype(jnp.bfloat16), standing.astype(jnp.bfloat16)

    new_all, standing_all = lax.map(one_replica, jnp.arange(group_count * node_count, dtype=jnp.int32))
    new_context = new_all.reshape((group_count, node_count) + new_all.shape[1:])
    resident_context = standing_all.reshape((group_count, node_count) + standing_all.shape[1:])
    return new_context, resident_context
```

```python
import functools

import jax
import jax.numpy as jnp
from jax import lax
from jax.experimental import pallas as pl
from jax.experimental.pallas import tpu as pltpu
from jax.sharding import Mesh
from jax.sharding import PartitionSpec as P

LATENT = 512
LANES = 128
score_scale = 1.0 / 192.0**0.5

SMEM = pl.BlockSpec(memory_space=pltpu.SMEM)
VMEM = pl.BlockSpec(memory_space=pltpu.VMEM)


def dot_rows(left, right):
    return lax.dot_general(
        left, right, (((1,), (1,)), ((), ())), preferred_element_type=jnp.float32
    )


def dot_plain(left, right):
    return lax.dot_general(
        left, right, (((1,), (0,)), ((), ())), preferred_element_type=jnp.float32
    )


def pad_rows(rows, count):
    wide = rows.astype(jnp.float32)
    below = jnp.zeros((count - rows.shape[0], rows.shape[1]), jnp.float32)
    return jnp.concatenate([wide, below], axis=0).astype(jnp.bfloat16)


def own_mask(rows, columns, heads, steps):
    step = (lax.broadcasted_iota(jnp.int32, (rows, columns), 0) // heads) % steps
    return lax.broadcasted_iota(jnp.int32, (rows, columns), 1) <= step


def resident_kernel(heads, lengths, queries, keys_t, own, out):
    rows = queries.shape[1]
    for b in range(queries.shape[0]):
        q = queries[b]
        scores = dot_plain(q, keys_t[b]) * score_scale
        position = lax.broadcasted_iota(jnp.int32, (1, scores.shape[1]), 1)
        scores = jnp.where(position < lengths[b], scores, -jnp.inf)
        own_rows = pad_rows(own[b], 8)
        own_scores = dot_rows(q, own_rows) * score_scale
        seen = own_mask(rows, 8, heads, own.shape[1])
        own_scores = jnp.where(seen, own_scores, -jnp.inf)
        top = jnp.maximum(
            jnp.max(scores, axis=1, keepdims=True), jnp.max(own_scores, axis=1, keepdims=True)
        )
        e = jnp.exp(scores - top)
        own_e = jnp.exp(own_scores - top)
        total = jnp.sum(e, axis=1, keepdims=True) + jnp.sum(own_e, axis=1, keepdims=True)
        sums = dot_rows(e.astype(jnp.bfloat16), keys_t[b, :LATENT, :])
        sums = sums + dot_plain(own_e.astype(jnp.bfloat16), own_rows[:, :LATENT])
        out[b] = (sums / total).astype(jnp.bfloat16)


def place_kernel(per, plan, first, second, out):
    prompts = first.shape[0]
    for dest in range(out.shape[0]):
        rotary = []
        for j in range(per):
            pick = plan[dest * per + j]
            at = pick % prompts
            block = jnp.where(pick < prompts, first[at], second[at])
            out[dest, :, j * LATENT : (j + 1) * LATENT] = block[:, :LATENT]
            rotary.append(block[:, LATENT:])
        out[dest, :, per * LATENT :] = jnp.concatenate(rotary, axis=1)


def slot_kernel(per, chunk, heads, steps, plan, queries, kv, own, out, held, sems):
    blocks = queries.shape[0]
    rows = blocks * queries.shape[2]
    rotary = queries.shape[3] - LATENT
    column = lax.broadcasted_iota(jnp.int32, (1, kv.shape[0]), 1)
    came_by = column // chunk
    copies = []
    for j in range(per):
        length = plan[blocks * per + j]
        turn = plan[blocks * per + per + j]
        q = queries[:, j].reshape(rows, queries.shape[3])
        blank = jnp.zeros((rows, rotary), jnp.bfloat16)
        q_rotary = jnp.concatenate([blank] * j + [q[:, LATENT:]] + [blank] * (per - 1 - j), axis=1)
        latents = kv[:, j * LATENT : (j + 1) * LATENT]
        scores = dot_rows(q[:, :LATENT], latents) + dot_rows(q_rotary, kv[:, per * LATENT :])
        source_chip = (turn + blocks - came_by) % blocks
        position = source_chip * chunk + (column - came_by * chunk)
        scores = jnp.where(position < length, scores * score_scale, -jnp.inf)
        own_rows = own[j]
        own_scores = dot_rows(q, own_rows) * score_scale
        own_scores = jnp.where(
            own_mask(rows, own.shape[1], heads, steps), own_scores, -jnp.inf
        )
        top = jnp.maximum(
            jnp.max(scores, axis=1, keepdims=True), jnp.max(own_scores, axis=1, keepdims=True)
        )
        e = jnp.exp(scores - top)
        own_e = jnp.exp(own_scores - top)
        total = jnp.sum(e, axis=1, keepdims=True) + jnp.sum(own_e, axis=1, keepdims=True)
        sums = dot_plain(e.astype(jnp.bfloat16), latents)
        sums = sums + dot_plain(own_e.astype(jnp.bfloat16), own_rows[:, :LATENT])
        context = jnp.where(length > 0, sums / total, 0.0).astype(jnp.bfloat16)
        held[j] = context.reshape(blocks, queries.shape[2], LATENT)
        copies.append(pltpu.make_async_copy(held.at[j], out.at[:, j], sems.at[j]))
        copies[-1].start()
    for copy in copies:
        copy.wait()


def call(kernel, shape, in_specs, *operands, out_specs=VMEM, scratch=()):
    return pl.pallas_call(
        kernel,
        out_shape=jax.ShapeDtypeStruct(shape, jnp.bfloat16),
        in_specs=in_specs,
        out_specs=out_specs,
        scratch_shapes=scratch,
        compiler_params=pltpu.CompilerParams(vmem_limit_bytes=40 * 2**20),
    )(*operands)


def plan_of(sizes, lengths, replica):
    groups, halves, ys, chips = sizes
    per = halves * ys // chips
    source_group = (lax.axis_index("group") + groups // 2) % groups
    half, here, chip = lax.axis_index("xh"), lax.axis_index("y"), lax.axis_index("chip")
    prompts = replica.shape[2]
    start, size = (source_group, chip * per, 0), (1, per, prompts)
    to = lax.dynamic_slice(replica, start, size)
    long = lax.dynamic_slice(lengths, start, size)
    target = half * ys + lax.broadcasted_iota(jnp.int32, (ys, per, prompts), 0)
    turn = (half + lax.broadcasted_iota(jnp.int32, (ys, per, prompts), 1)) % halves
    which = lax.broadcasted_iota(jnp.int32, (ys, per, prompts), 2)
    pick = jnp.sum(jnp.where(to == target, which, 0), axis=2) + turn[:, :, 0] * prompts
    held = jnp.sum(jnp.where(to[0] == half * ys + here, long[0], 0), axis=1)
    slot = chip * per + lax.broadcasted_iota(jnp.int32, (per,), 0)
    return jnp.concatenate([pick.reshape(-1), held, (slot + slot // per) % ys])


def hand_over_pairs(groups, halves, ys, chips, turn):
    per = halves * ys // chips
    pairs = []
    for group in range(groups):
        for half in range(halves):
            for y in range(ys):
                for chip in range(chips):
                    node = half * ys + y
                    to = (
                        (group + groups // 2) % groups,
                        (node + turn) % halves,
                        (node + node // per - chip) % ys,
                        node // per,
                    )
                    pairs.append((
                        ((group * halves + half) * ys + y) * chips + chip,
                        ((to[0] * halves + to[1]) * ys + to[2]) * chips + to[3],
                    ))
    return pairs


def on_device(
    sizes,
    prompt_cache,
    prompt_lengths,
    prompt_replica,
    new_queries,
    new_rows,
    resident_cache,
    resident_queries,
    resident_rows,
    resident_lengths,
):
    groups, halves, ys, chips = sizes
    per = halves * ys // chips
    slots, steps, heads, width = new_queries.shape[2:]
    prompts, chunk = prompt_cache.shape[2:4]
    axes = ("group", "xh", "y", "chip")
    first, second = [
        lax.ppermute(prompt_cache[0, 0], axes, hand_over_pairs(*sizes, turn)) for turn in range(2)
    ]
    queries = lax.all_to_all(new_queries[0, 0], "chip", split_axis=0, concat_axis=0, tiled=True)
    queries = queries.reshape(chips, per, steps * heads, width)
    plan = plan_of(sizes, prompt_lengths, prompt_replica)
    own = lax.dynamic_slice_in_dim(new_rows[0, 0], lax.axis_index("chip") * per, per, 0)
    own = jnp.pad(own, ((0, 0), (0, 8 - steps), (0, 0)))
    queries, plan, own = lax.optimization_barrier((queries, plan, own))

    sequences = resident_queries.shape[2]
    resident = call(
        functools.partial(resident_kernel, heads),
        (sequences, steps * heads, LATENT),
        [SMEM, VMEM, VMEM, VMEM],
        resident_lengths.reshape(sequences),
        resident_queries.reshape(sequences, steps * heads, width),
        jnp.swapaxes(resident_cache[0, 0], 1, 2),
        resident_rows[0, 0],
    )

    outgoing = call(
        functools.partial(place_kernel, per),
        (ys, chunk, per * width),
        [SMEM, VMEM, VMEM],
        plan,
        first,
        second,
    )
    kv = lax.all_to_all(outgoing, "y", split_axis=0, concat_axis=0, tiled=True)
    kv = kv.reshape(ys * chunk, per * width)
    context = call(
        functools.partial(slot_kernel, per, chunk, heads, steps),
        (chips, per, steps * heads, LATENT),
        [SMEM, VMEM, VMEM, VMEM],
        plan,
        queries,
        kv,
        own,
        out_specs=pl.BlockSpec(memory_space=pltpu.MemorySpace.HBM),
        scratch=[
            pltpu.VMEM((per, chips, steps * heads, LATENT), jnp.bfloat16),
            pltpu.SemaphoreType.DMA((per,)),
        ],
    )
    context = context.reshape(1, 1, slots, steps, heads, LATENT)
    new_context = lax.all_to_all(context, "chip", split_axis=2, concat_axis=2, tiled=True)
    resident_context = resident.reshape(1, 1, sequences, steps, heads, LATENT)
    return (new_context, resident_context)


def solution(mesh):
    groups, nodes, chips = mesh.devices.shape
    halves = 2
    sizes = (groups, halves, nodes // halves, chips)
    fine = Mesh(mesh.devices.reshape(sizes), ("group", "xh", "y", "chip"))
    node = ("xh", "y")
    in_specs = (
        P("group", node, None, "chip", None),
        P(),
        P(),
        P("group", node, None, None, "chip", None),
        P("group", node, None, None, None),
        P("group", node, None, None, None),
        P("group", node, None, None, "chip", None),
        P("group", node, None, None, None),
        P("group", node, None),
    )
    out_specs = (
        P("group", node, None, None, "chip", None),
        P("group", node, None, None, "chip", None),
    )
    return jax.shard_map(
        functools.partial(on_device, sizes),
        mesh=fine,
        in_specs=in_specs,
        out_specs=out_specs,
        check_vma=False,
    )
```

```python
import functools

import jax
import jax.numpy as jnp
from jax import lax
from jax.experimental import pallas as pl
from jax.experimental.pallas import tpu as pltpu
from jax.sharding import Mesh
from jax.sharding import PartitionSpec as P

LATENT = 512
LANES = 128
score_scale = 1.0 / 192.0**0.5

SMEM = pl.BlockSpec(memory_space=pltpu.SMEM)
VMEM = pl.BlockSpec(memory_space=pltpu.VMEM)


def dot_rows(left, right):
    return lax.dot_general(
        left, right, (((1,), (1,)), ((), ())), preferred_element_type=jnp.float32
    )


def dot_plain(left, right):
    return lax.dot_general(
        left, right, (((1,), (0,)), ((), ())), preferred_element_type=jnp.float32
    )


def pad_rows(rows, count):
    wide = rows.astype(jnp.float32)
    below = jnp.zeros((count - rows.shape[0], rows.shape[1]), jnp.float32)
    return jnp.concatenate([wide, below], axis=0).astype(jnp.bfloat16)


def own_mask(rows, columns, heads, steps):
    step = (lax.broadcasted_iota(jnp.int32, (rows, columns), 0) // heads) % steps
    return lax.broadcasted_iota(jnp.int32, (rows, columns), 1) <= step


def resident_kernel(heads, lengths, queries, keys_t, own, out):
    rows = queries.shape[1]
    for b in range(queries.shape[0]):
        q = queries[b]
        scores = dot_plain(q, keys_t[b]) * score_scale
        position = lax.broadcasted_iota(jnp.int32, (1, scores.shape[1]), 1)
        scores = jnp.where(position < lengths[b], scores, -jnp.inf)
        own_rows = pad_rows(own[b], 8)
        own_scores = dot_rows(q, own_rows) * score_scale
        seen = own_mask(rows, 8, heads, own.shape[1])
        own_scores = jnp.where(seen, own_scores, -jnp.inf)
        top = jnp.maximum(
            jnp.max(scores, axis=1, keepdims=True), jnp.max(own_scores, axis=1, keepdims=True)
        )
        e = jnp.exp(scores - top)
        own_e = jnp.exp(own_scores - top)
        total = jnp.sum(e, axis=1, keepdims=True) + jnp.sum(own_e, axis=1, keepdims=True)
        sums = dot_rows(e.astype(jnp.bfloat16), keys_t[b, :LATENT, :])
        sums = sums + dot_plain(own_e.astype(jnp.bfloat16), own_rows[:, :LATENT])
        out[b] = (sums / total).astype(jnp.bfloat16)


def place_kernel(per, plan, first, second, out):
    prompts = first.shape[0]
    for dest in range(out.shape[0]):
        rotary = []
        for j in range(per):
            pick = plan[dest * per + j]
            at = pick % prompts
            block = jnp.where(pick < prompts, first[at], second[at])
            out[dest, :, j * LATENT : (j + 1) * LATENT] = block[:, :LATENT]
            rotary.append(block[:, LATENT:])
        out[dest, :, per * LATENT :] = jnp.concatenate(rotary, axis=1)


def slot_kernel(per, chunk, heads, steps, plan, queries, kv, own, out, held, sems):
    blocks = queries.shape[0]
    rows = blocks * queries.shape[2]
    rotary = queries.shape[3] - LATENT
    column = lax.broadcasted_iota(jnp.int32, (1, kv.shape[0]), 1)
    came_by = column // chunk
    copies = []
    for j in range(per):
        length = plan[blocks * per + j]
        turn = plan[blocks * per + per + j]
        q = queries[:, j].reshape(rows, queries.shape[3])
        blank = jnp.zeros((rows, rotary), jnp.bfloat16)
        q_rotary = jnp.concatenate([blank] * j + [q[:, LATENT:]] + [blank] * (per - 1 - j), axis=1)
        latents = kv[:, j * LATENT : (j + 1) * LATENT]
        scores = dot_rows(q[:, :LATENT], latents) + dot_rows(q_rotary, kv[:, per * LATENT :])
        source_chip = (turn + blocks - came_by) % blocks
        position = source_chip * chunk + (column - came_by * chunk)
        scores = jnp.where(position < length, scores * score_scale, -jnp.inf)
        own_rows = own[j]
        own_scores = dot_rows(q, own_rows) * score_scale
        own_scores = jnp.where(
            own_mask(rows, own.shape[1], heads, steps), own_scores, -jnp.inf
        )
        top = jnp.maximum(
            jnp.max(scores, axis=1, keepdims=True), jnp.max(own_scores, axis=1, keepdims=True)
        )
        e = jnp.exp(scores - top)
        own_e = jnp.exp(own_scores - top)
        total = jnp.sum(e, axis=1, keepdims=True) + jnp.sum(own_e, axis=1, keepdims=True)
        sums = dot_plain(e.astype(jnp.bfloat16), latents)
        sums = sums + dot_plain(own_e.astype(jnp.bfloat16), own_rows[:, :LATENT])
        context = jnp.where(length > 0, sums / total, 0.0).astype(jnp.bfloat16)
        held[j] = context.reshape(blocks, queries.shape[2], LATENT)
        copies.append(pltpu.make_async_copy(held.at[j], out.at[:, j], sems.at[j]))
        copies[-1].start()
    for copy in copies:
        copy.wait()


def call(kernel, shape, in_specs, *operands, out_specs=VMEM, scratch=()):
    return pl.pallas_call(
        kernel,
        out_shape=jax.ShapeDtypeStruct(shape, jnp.bfloat16),
        in_specs=in_specs,
        out_specs=out_specs,
        scratch_shapes=scratch,
        compiler_params=pltpu.CompilerParams(vmem_limit_bytes=40 * 2**20),
    )(*operands)


def plan_of(sizes, lengths, replica):
    groups, halves, ys, chips = sizes
    per = halves * ys // chips
    source_group = (lax.axis_index("group") + groups // 2) % groups
    half, here, chip = lax.axis_index("xh"), lax.axis_index("y"), lax.axis_index("chip")
    prompts = replica.shape[2]
    start, size = (source_group, chip * per, 0), (1, per, prompts)
    to = lax.dynamic_slice(replica, start, size)
    long = lax.dynamic_slice(lengths, start, size)
    target = half * ys + lax.broadcasted_iota(jnp.int32, (ys, per, prompts), 0)
    turn = (half + lax.broadcasted_iota(jnp.int32, (ys, per, prompts), 1)) % halves
    which = lax.broadcasted_iota(jnp.int32, (ys, per, prompts), 2)
    pick = jnp.sum(jnp.where(to == target, which, 0), axis=2) + turn[:, :, 0] * prompts
    held = jnp.sum(jnp.where(to[0] == half * ys + here, long[0], 0), axis=1)
    slot = chip * per + lax.broadcasted_iota(jnp.int32, (per,), 0)
    return jnp.concatenate([pick.reshape(-1), held, (slot + slot // per) % ys])


def hand_over_pairs(groups, halves, ys, chips, turn):
    per = halves * ys // chips
    pairs = []
    for group in range(groups):
        for half in range(halves):
            for y in range(ys):
                for chip in range(chips):
                    node = half * ys + y
                    to = (
                        (group + groups // 2) % groups,
                        (node + turn) % halves,
                        (node + node // per - chip) % ys,
                        node // per,
                    )
                    pairs.append((
                        ((group * halves + half) * ys + y) * chips + chip,
                        ((to[0] * halves + to[1]) * ys + to[2]) * chips + to[3],
                    ))
    return pairs


def on_device(
    sizes,
    prompt_cache,
    prompt_lengths,
    prompt_replica,
    new_queries,
    new_rows,
    resident_cache,
    resident_queries,
    resident_rows,
    resident_lengths,
):
    groups, halves, ys, chips = sizes
    per = halves * ys // chips
    slots, steps, heads, width = new_queries.shape[2:]
    prompts, chunk = prompt_cache.shape[2:4]
    axes = ("group", "xh", "y", "chip")
    plan = plan_of(sizes, prompt_lengths, prompt_replica)
    own = lax.dynamic_slice_in_dim(new_rows[0, 0], lax.axis_index("chip") * per, per, 0)
    own = jnp.pad(own, ((0, 0), (0, 8 - steps), (0, 0)))
    plan, own, prompt_cache = lax.optimization_barrier((plan, own, prompt_cache))
    first, second = [
        lax.ppermute(prompt_cache[0, 0], axes, hand_over_pairs(*sizes, turn)) for turn in range(2)
    ]
    queries = lax.all_to_all(new_queries[0, 0], "chip", split_axis=0, concat_axis=0, tiled=True)
    queries = queries.reshape(chips, per, steps * heads, width)
    queries, plan = lax.optimization_barrier((queries, plan))

    sequences = resident_queries.shape[2]
    resident = call(
        functools.partial(resident_kernel, heads),
        (sequences, steps * heads, LATENT),
        [SMEM, VMEM, VMEM, VMEM],
        resident_lengths.reshape(sequences),
        resident_queries.reshape(sequences, steps * heads, width),
        jnp.swapaxes(resident_cache[0, 0], 1, 2),
        resident_rows[0, 0],
    )

    outgoing = call(
        functools.partial(place_kernel, per),
        (ys, chunk, per * width),
        [SMEM, VMEM, VMEM],
        plan,
        first,
        second,
    )
    kv = lax.all_to_all(outgoing, "y", split_axis=0, concat_axis=0, tiled=True)
    kv = kv.reshape(ys * chunk, per * width)
    context = call(
        functools.partial(slot_kernel, per, chunk, heads, steps),
        (chips, per, steps * heads, LATENT),
        [SMEM, VMEM, VMEM, VMEM],
        plan,
        queries,
        kv,
        own,
        out_specs=pl.BlockSpec(memory_space=pltpu.MemorySpace.HBM),
        scratch=[
            pltpu.VMEM((per, chips, steps * heads, LATENT), jnp.bfloat16),
            pltpu.SemaphoreType.DMA((per,)),
        ],
    )
    context = context.reshape(1, 1, slots, steps, heads, LATENT)
    new_context = lax.all_to_all(context, "chip", split_axis=2, concat_axis=2, tiled=True)
    resident_context = resident.reshape(1, 1, sequences, steps, heads, LATENT)
    return (new_context, resident_context)


def solution(mesh):
    groups, nodes, chips = mesh.devices.shape
    halves = 2
    sizes = (groups, halves, nodes // halves, chips)
    fine = Mesh(mesh.devices.reshape(sizes), ("group", "xh", "y", "chip"))
    node = ("xh", "y")
    in_specs = (
        P("group", node, None, "chip", None),
        P(),
        P(),
        P("group", node, None, None, "chip", None),
        P("group", node, None, None, None),
        P("group", node, None, None, None),
        P("group", node, None, None, "chip", None),
        P("group", node, None, None, None),
        P("group", node, None),
    )
    out_specs = (
        P("group", node, None, None, "chip", None),
        P("group", node, None, None, "chip", None),
    )
    return jax.shard_map(
        functools.partial(on_device, sizes),
        mesh=fine,
        in_specs=in_specs,
        out_specs=out_specs,
        check_vma=False,
    )
```

```python
import functools

import jax
import jax.numpy as jnp
from jax import lax
from jax.experimental import pallas as pl
from jax.experimental.pallas import tpu as pltpu
from jax.sharding import Mesh
from jax.sharding import PartitionSpec as P

LATENT = 512
LANES = 128
score_scale = 1.0 / 192.0**0.5

SMEM = pl.BlockSpec(memory_space=pltpu.SMEM)
VMEM = pl.BlockSpec(memory_space=pltpu.VMEM)


def dot_rows(left, right):
    return lax.dot_general(
        left, right, (((1,), (1,)), ((), ())), preferred_element_type=jnp.float32
    )


def dot_plain(left, right):
    return lax.dot_general(
        left, right, (((1,), (0,)), ((), ())), preferred_element_type=jnp.float32
    )


def pad_rows(rows, count):
    wide = rows.astype(jnp.float32)
    below = jnp.zeros((count - rows.shape[0], rows.shape[1]), jnp.float32)
    return jnp.concatenate([wide, below], axis=0).astype(jnp.bfloat16)


def own_mask(rows, columns, heads, steps):
    step = (lax.broadcasted_iota(jnp.int32, (rows, columns), 0) // heads) % steps
    return lax.broadcasted_iota(jnp.int32, (rows, columns), 1) <= step


def resident_kernel(heads, lengths, queries, keys_t, own, out):
    rows = queries.shape[1]
    for b in range(queries.shape[0]):
        q = queries[b]
        scores = dot_plain(q, keys_t[b]) * score_scale
        position = lax.broadcasted_iota(jnp.int32, (1, scores.shape[1]), 1)
        scores = jnp.where(position < lengths[b], scores, -jnp.inf)
        own_rows = pad_rows(own[b], 8)
        own_scores = dot_rows(q, own_rows) * score_scale
        seen = own_mask(rows, 8, heads, own.shape[1])
        own_scores = jnp.where(seen, own_scores, -jnp.inf)
        top = jnp.maximum(
            jnp.max(scores, axis=1, keepdims=True), jnp.max(own_scores, axis=1, keepdims=True)
        )
        e = jnp.exp(scores - top)
        own_e = jnp.exp(own_scores - top)
        total = jnp.sum(e, axis=1, keepdims=True) + jnp.sum(own_e, axis=1, keepdims=True)
        sums = dot_rows(e.astype(jnp.bfloat16), keys_t[b, :LATENT, :])
        sums = sums + dot_plain(own_e.astype(jnp.bfloat16), own_rows[:, :LATENT])
        out[b] = (sums * (1.0 / total)).astype(jnp.bfloat16)


def place_kernel(per, plan, first, second, out):
    prompts = first.shape[0]
    for dest in range(out.shape[0]):
        rotary = []
        for j in range(per):
            pick = plan[dest * per + j]
            at = pick % prompts
            block = jnp.where(pick < prompts, first[at], second[at])
            out[dest, :, j * LATENT : (j + 1) * LATENT] = block[:, :LATENT]
            rotary.append(block[:, LATENT:])
        out[dest, :, per * LATENT :] = jnp.concatenate(rotary, axis=1)


def slot_kernel(per, chunk, heads, steps, plan, queries, kv, own, out, held, sems):
    blocks = queries.shape[0]
    rows = blocks * queries.shape[2]
    rotary = queries.shape[3] - LATENT
    cached = kv.shape[0]
    count = cached + own.shape[1]
    column = lax.broadcasted_iota(jnp.int32, (1, count), 1)
    came_by = column // chunk
    step = (lax.broadcasted_iota(jnp.int32, (rows, 1), 0) // heads) % steps
    own_rotary = jnp.concatenate([own[j, :, LATENT:] for j in range(per)], axis=1)
    key_rotary = jnp.concatenate([kv[:, per * LATENT :], own_rotary], axis=0)
    copies = []
    for j in range(per):
        length = plan[blocks * per + j]
        turn = plan[blocks * per + per + j]
        q = queries[:, j].reshape(rows, queries.shape[3])
        blank = jnp.zeros((rows, rotary), jnp.bfloat16)
        q_rotary = jnp.concatenate([blank] * j + [q[:, LATENT:]] + [blank] * (per - 1 - j), axis=1)
        latents = jnp.concatenate(
            [kv[:, j * LATENT : (j + 1) * LATENT], own[j, :, :LATENT]], axis=0
        )
        scores = dot_rows(q[:, :LATENT], latents) + dot_rows(q_rotary, key_rotary)
        source_chip = (turn + blocks - came_by) % blocks
        position = source_chip * chunk + (column - came_by * chunk)
        position = jnp.where(column < cached, position, column - cached)
        bound = jnp.where(column < cached, length, step + 1)
        scores = jnp.where(position < bound, scores * score_scale, -jnp.inf)
        top = jnp.max(scores, axis=1, keepdims=True)
        e = jnp.exp(scores - top)
        total = jnp.sum(e, axis=1, keepdims=True)
        sums = dot_plain(e.astype(jnp.bfloat16), latents)
        share = jnp.where(length > 0, 1.0 / total, 0.0)
        held[j] = (sums * share).astype(jnp.bfloat16).reshape(blocks, queries.shape[2], LATENT)
        copies.append(pltpu.make_async_copy(held.at[j], out.at[:, j], sems.at[j]))
        copies[-1].start()
    for copy in copies:
        copy.wait()


def call(kernel, shape, in_specs, *operands, out_specs=VMEM, scratch=()):
    return pl.pallas_call(
        kernel,
        out_shape=jax.ShapeDtypeStruct(shape, jnp.bfloat16),
        in_specs=in_specs,
        out_specs=out_specs,
        scratch_shapes=scratch,
        compiler_params=pltpu.CompilerParams(vmem_limit_bytes=40 * 2**20),
    )(*operands)


def plan_of(sizes, lengths, replica):
    groups, halves, ys, chips = sizes
    per = halves * ys // chips
    source_group = (lax.axis_index("group") + groups // 2) % groups
    half, here, chip = lax.axis_index("xh"), lax.axis_index("y"), lax.axis_index("chip")
    prompts = replica.shape[2]
    start, size = (source_group, chip * per, 0), (1, per, prompts)
    to = lax.dynamic_slice(replica, start, size)
    long = lax.dynamic_slice(lengths, start, size)
    target = half * ys + lax.broadcasted_iota(jnp.int32, (ys, per, prompts), 0)
    turn = (half + lax.broadcasted_iota(jnp.int32, (ys, per, prompts), 1)) % halves
    which = lax.broadcasted_iota(jnp.int32, (ys, per, prompts), 2)
    pick = jnp.sum(jnp.where(to == target, which, 0), axis=2) + turn[:, :, 0] * prompts
    held = jnp.sum(jnp.where(to[0] == half * ys + here, long[0], 0), axis=1)
    slot = chip * per + lax.broadcasted_iota(jnp.int32, (per,), 0)
    return jnp.concatenate([pick.reshape(-1), held, (slot + slot // per + 4) % ys])


def hand_over_pairs(groups, halves, ys, chips, turn):
    per = halves * ys // chips
    pairs = []
    for group in range(groups):
        for half in range(halves):
            for y in range(ys):
                for chip in range(chips):
                    node = half * ys + y
                    to = (
                        (group + groups // 2) % groups,
                        (node + turn) % halves,
                        (node + node // per + 4 - chip) % ys,
                        node // per,
                    )
                    pairs.append((
                        ((group * halves + half) * ys + y) * chips + chip,
                        ((to[0] * halves + to[1]) * ys + to[2]) * chips + to[3],
                    ))
    return pairs


def on_device(
    sizes,
    prompt_cache,
    prompt_lengths,
    prompt_replica,
    new_queries,
    new_rows,
    resident_cache,
    resident_queries,
    resident_rows,
    resident_lengths,
):
    groups, halves, ys, chips = sizes
    per = halves * ys // chips
    slots, steps, heads, width = new_queries.shape[2:]
    prompts, chunk = prompt_cache.shape[2:4]
    axes = ("group", "xh", "y", "chip")
    plan = plan_of(sizes, prompt_lengths, prompt_replica)
    own = lax.dynamic_slice_in_dim(new_rows[0, 0], lax.axis_index("chip") * per, per, 0)
    own = jnp.pad(own, ((0, 0), (0, 16 - steps), (0, 0)))
    plan, own, prompt_cache = lax.optimization_barrier((plan, own, prompt_cache))
    first, second = [
        lax.ppermute(prompt_cache[0, 0], axes, hand_over_pairs(*sizes, turn)) for turn in range(2)
    ]
    queries = lax.all_to_all(new_queries[0, 0], "chip", split_axis=0, concat_axis=0, tiled=True)
    queries = queries.reshape(chips, per, steps * heads, width)
    queries, plan = lax.optimization_barrier((queries, plan))

    sequences = resident_queries.shape[2]
    resident = call(
        functools.partial(resident_kernel, heads),
        (sequences, steps * heads, LATENT),
        [SMEM, VMEM, VMEM, VMEM],
        resident_lengths.reshape(sequences),
        resident_queries.reshape(sequences, steps * heads, width),
        jnp.swapaxes(resident_cache[0, 0], 1, 2),
        resident_rows[0, 0],
    )

    outgoing = call(
        functools.partial(place_kernel, per),
        (ys, chunk, per * width),
        [SMEM, VMEM, VMEM],
        plan,
        first,
        second,
    )
    kv = lax.all_to_all(outgoing, "y", split_axis=0, concat_axis=0, tiled=True)
    kv = kv.reshape(ys * chunk, per * width)
    context = call(
        functools.partial(slot_kernel, per, chunk, heads, steps),
        (chips, per, steps * heads, LATENT),
        [SMEM, VMEM, VMEM, VMEM],
        plan,
        queries,
        kv,
        own,
        out_specs=pl.BlockSpec(memory_space=pltpu.MemorySpace.HBM),
        scratch=[
            pltpu.VMEM((per, chips, steps * heads, LATENT), jnp.bfloat16),
            pltpu.SemaphoreType.DMA((per,)),
        ],
    )
    context = context.reshape(1, 1, slots, steps, heads, LATENT)
    new_context = lax.all_to_all(context, "chip", split_axis=2, concat_axis=2, tiled=True)
    resident_context = resident.reshape(1, 1, sequences, steps, heads, LATENT)
    return (new_context, resident_context)


def solution(mesh):
    groups, nodes, chips = mesh.devices.shape
    halves = 2
    sizes = (groups, halves, nodes // halves, chips)
    fine = Mesh(mesh.devices.reshape(sizes), ("group", "xh", "y", "chip"))
    node = ("xh", "y")
    in_specs = (
        P("group", node, None, "chip", None),
        P(),
        P(),
        P("group", node, None, None, "chip", None),
        P("group", node, None, None, None),
        P("group", node, None, None, None),
        P("group", node, None, None, "chip", None),
        P("group", node, None, None, None),
        P("group", node, None),
    )
    out_specs = (
        P("group", node, None, None, "chip", None),
        P("group", node, None, None, "chip", None),
    )
    return jax.shard_map(
        functools.partial(on_device, sizes),
        mesh=fine,
        in_specs=in_specs,
        out_specs=out_specs,
        check_vma=False,
    )
```

```python
import functools

import jax
import jax.numpy as jnp
from jax import lax
from jax.experimental import pallas as pl
from jax.experimental.pallas import tpu as pltpu
from jax.sharding import Mesh
from jax.sharding import PartitionSpec as P

LATENT = 512
LANES = 128
score_scale = 1.0 / 192.0**0.5

SMEM = pl.BlockSpec(memory_space=pltpu.SMEM)
VMEM = pl.BlockSpec(memory_space=pltpu.VMEM)


def dot_rows(left, right):
    return lax.dot_general(
        left, right, (((1,), (1,)), ((), ())), preferred_element_type=jnp.float32
    )


def dot_plain(left, right):
    return lax.dot_general(
        left, right, (((1,), (0,)), ((), ())), preferred_element_type=jnp.float32
    )


def pad_rows(rows, count):
    wide = rows.astype(jnp.float32)
    below = jnp.zeros((count - rows.shape[0], rows.shape[1]), jnp.float32)
    return jnp.concatenate([wide, below], axis=0).astype(jnp.bfloat16)


def own_mask(rows, columns, heads, steps):
    step = (lax.broadcasted_iota(jnp.int32, (rows, columns), 0) // heads) % steps
    return lax.broadcasted_iota(jnp.int32, (rows, columns), 1) <= step


def resident_kernel(heads, lengths, queries, keys_t, own, out):
    rows = queries.shape[1]
    for b in range(queries.shape[0]):
        q = queries[b]
        scores = dot_plain(q, keys_t[b]) * score_scale
        position = lax.broadcasted_iota(jnp.int32, (1, scores.shape[1]), 1)
        scores = jnp.where(position < lengths[b], scores, -jnp.inf)
        own_rows = pad_rows(own[b], 8)
        own_scores = dot_rows(q, own_rows) * score_scale
        seen = own_mask(rows, 8, heads, own.shape[1])
        own_scores = jnp.where(seen, own_scores, -jnp.inf)
        top = jnp.maximum(
            jnp.max(scores, axis=1, keepdims=True), jnp.max(own_scores, axis=1, keepdims=True)
        )
        e = jnp.exp(scores - top)
        own_e = jnp.exp(own_scores - top)
        total = jnp.sum(e, axis=1, keepdims=True) + jnp.sum(own_e, axis=1, keepdims=True)
        sums = dot_rows(e.astype(jnp.bfloat16), keys_t[b, :LATENT, :])
        sums = sums + dot_plain(own_e.astype(jnp.bfloat16), own_rows[:, :LATENT])
        out[b] = (sums * (1.0 / total)).astype(jnp.bfloat16)


def place_kernel(per, plan, first, second, out):
    prompts = first.shape[0]
    for dest in range(out.shape[0]):
        rotary = []
        for j in range(per):
            pick = plan[dest * per + j]
            at = pick % prompts
            block = jnp.where(pick < prompts, first[at], second[at])
            out[dest, :, j * LATENT : (j + 1) * LATENT] = block[:, :LATENT]
            rotary.append(block[:, LATENT:])
        out[dest, :, per * LATENT :] = jnp.concatenate(rotary, axis=1)


def slot_kernel(per, chunk, heads, steps, plan, queries, kv, own, out, held, sems):
    blocks = queries.shape[0]
    rows = blocks * queries.shape[2]
    rotary = queries.shape[3] - LATENT
    cached = kv.shape[0]
    count = cached + own.shape[1]
    column = lax.broadcasted_iota(jnp.int32, (1, count), 1)
    came_by = column // chunk
    step = (lax.broadcasted_iota(jnp.int32, (rows, 1), 0) // heads) % steps
    own_rotary = jnp.concatenate([own[j, :, LATENT:] for j in range(per)], axis=1)
    key_rotary = jnp.concatenate([kv[:, per * LATENT :], own_rotary], axis=0)
    copies = []
    for j in range(per):
        length = plan[blocks * per + j]
        turn = plan[blocks * per + per + j]
        q = queries[:, j].reshape(rows, queries.shape[3])
        blank = jnp.zeros((rows, rotary), jnp.bfloat16)
        q_rotary = jnp.concatenate([blank] * j + [q[:, LATENT:]] + [blank] * (per - 1 - j), axis=1)
        latents = jnp.concatenate(
            [kv[:, j * LATENT : (j + 1) * LATENT], own[j, :, :LATENT]], axis=0
        )
        scores = dot_rows(q[:, :LATENT], latents) + dot_rows(q_rotary, key_rotary)
        source_chip = (turn + came_by) % blocks
        position = source_chip * chunk + (column - came_by * chunk)
        position = jnp.where(column < cached, position, column - cached)
        bound = jnp.where(column < cached, length, step + 1)
        scores = jnp.where(position < bound, scores * score_scale, -jnp.inf)
        top = jnp.max(scores, axis=1, keepdims=True)
        e = jnp.exp(scores - top)
        total = jnp.sum(e, axis=1, keepdims=True)
        sums = dot_plain(e.astype(jnp.bfloat16), latents)
        share = jnp.where(length > 0, 1.0 / total, 0.0)
        held[j] = (sums * share).astype(jnp.bfloat16).reshape(blocks, queries.shape[2], LATENT)
        copies.append(pltpu.make_async_copy(held.at[j], out.at[:, j], sems.at[j]))
        copies[-1].start()
    for copy in copies:
        copy.wait()


def call(kernel, shape, in_specs, *operands, out_specs=VMEM, scratch=()):
    return pl.pallas_call(
        kernel,
        out_shape=jax.ShapeDtypeStruct(shape, jnp.bfloat16),
        in_specs=in_specs,
        out_specs=out_specs,
        scratch_shapes=scratch,
        compiler_params=pltpu.CompilerParams(vmem_limit_bytes=40 * 2**20),
    )(*operands)


def plan_of(sizes, lengths, replica):
    groups, halves, ys, chips = sizes
    per = halves * ys // chips
    source_group = (lax.axis_index("group") + groups // 2) % groups
    half, here, chip = lax.axis_index("xh"), lax.axis_index("y"), lax.axis_index("chip")
    prompts = replica.shape[2]
    start, size = (source_group, chip * per, 0), (1, per, prompts)
    to = lax.dynamic_slice(replica, start, size)
    long = lax.dynamic_slice(lengths, start, size)
    target = half * ys + lax.broadcasted_iota(jnp.int32, (ys, per, prompts), 0)
    turn = (half + lax.broadcasted_iota(jnp.int32, (ys, per, prompts), 1)) % halves
    which = lax.broadcasted_iota(jnp.int32, (ys, per, prompts), 2)
    pick = jnp.sum(jnp.where(to == target, which, 0), axis=2) + turn[:, :, 0] * prompts
    held = jnp.sum(jnp.where(to[0] == half * ys + here, long[0], 0), axis=1)
    slot = chip * per + lax.broadcasted_iota(jnp.int32, (per,), 0)
    return jnp.concatenate([pick.reshape(-1), held, (slot // per + 4 - slot) % ys])


def hand_over_pairs(groups, halves, ys, chips, turn):
    per = halves * ys // chips
    pairs = []
    for group in range(groups):
        for half in range(halves):
            for y in range(ys):
                for chip in range(chips):
                    node = half * ys + y
                    to = (
                        (group + groups // 2) % groups,
                        (node + turn) % halves,
                        (node - node // per + 4 + chip) % ys,
                        node // per,
                    )
                    pairs.append((
                        ((group * halves + half) * ys + y) * chips + chip,
                        ((to[0] * halves + to[1]) * ys + to[2]) * chips + to[3],
                    ))
    return pairs


def on_device(
    sizes,
    prompt_cache,
    prompt_lengths,
    prompt_replica,
    new_queries,
    new_rows,
    resident_cache,
    resident_queries,
    resident_rows,
    resident_lengths,
):
    groups, halves, ys, chips = sizes
    per = halves * ys // chips
    slots, steps, heads, width = new_queries.shape[2:]
    prompts, chunk = prompt_cache.shape[2:4]
    axes = ("group", "xh", "y", "chip")
    plan = plan_of(sizes, prompt_lengths, prompt_replica)
    own = lax.dynamic_slice_in_dim(new_rows[0, 0], lax.axis_index("chip") * per, per, 0)
    own = jnp.pad(own, ((0, 0), (0, 16 - steps), (0, 0)))
    plan, own, prompt_cache = lax.optimization_barrier((plan, own, prompt_cache))
    first, second = [
        lax.ppermute(prompt_cache[0, 0], axes, hand_over_pairs(*sizes, turn)) for turn in range(2)
    ]
    queries = lax.all_to_all(new_queries[0, 0], "chip", split_axis=0, concat_axis=0, tiled=True)
    queries = queries.reshape(chips, per, steps * heads, width)
    queries, plan = lax.optimization_barrier((queries, plan))

    sequences = resident_queries.shape[2]
    resident = call(
        functools.partial(resident_kernel, heads),
        (sequences, steps * heads, LATENT),
        [SMEM, VMEM, VMEM, VMEM],
        resident_lengths.reshape(sequences),
        resident_queries.reshape(sequences, steps * heads, width),
        jnp.swapaxes(resident_cache[0, 0], 1, 2),
        resident_rows[0, 0],
    )

    outgoing = call(
        functools.partial(place_kernel, per),
        (ys, chunk, per * width),
        [SMEM, VMEM, VMEM],
        plan,
        first,
        second,
    )
    kv = lax.all_to_all(outgoing, "y", split_axis=0, concat_axis=0, tiled=True)
    kv = kv.reshape(ys * chunk, per * width)
    context = call(
        functools.partial(slot_kernel, per, chunk, heads, steps),
        (chips, per, steps * heads, LATENT),
        [SMEM, VMEM, VMEM, VMEM],
        plan,
        queries,
        kv,
        own,
        out_specs=pl.BlockSpec(memory_space=pltpu.MemorySpace.HBM),
        scratch=[
            pltpu.VMEM((per, chips, steps * heads, LATENT), jnp.bfloat16),
            pltpu.SemaphoreType.DMA((per,)),
        ],
    )
    context = context.reshape(1, 1, slots, steps, heads, LATENT)
    new_context = lax.all_to_all(context, "chip", split_axis=2, concat_axis=2, tiled=True)
    resident_context = resident.reshape(1, 1, sequences, steps, heads, LATENT)
    return (new_context, resident_context)


def solution(mesh):
    groups, nodes, chips = mesh.devices.shape
    halves = 2
    sizes = (groups, halves, nodes // halves, chips)
    fine = Mesh(mesh.devices.reshape(sizes), ("group", "xh", "y", "chip"))
    node = ("xh", "y")
    in_specs = (
        P("group", node, None, "chip", None),
        P(),
        P(),
        P("group", node, None, None, "chip", None),
        P("group", node, None, None, None),
        P("group", node, None, None, None),
        P("group", node, None, None, "chip", None),
        P("group", node, None, None, None),
        P("group", node, None),
    )
    out_specs = (
        P("group", node, None, None, "chip", None),
        P("group", node, None, None, "chip", None),
    )
    return jax.shard_map(
        functools.partial(on_device, sizes),
        mesh=fine,
        in_specs=in_specs,
        out_specs=out_specs,
        check_vma=False,
    )
```
